32 devices in a mesh: fsdp: 8 (over z, y), tp: 4 (over x, core).
Axes of the slice: x: 2, y: 2, z: 4, core: 2. Of those that a mesh axis runs over, the one named last changes fastest.
Arguments:
- llm_query: bfloat16 [8, 64, 8192], P('fsdp', None, 'tp'), may hold values from -15 to 15
- llm_kv: bfloat16 [8, 2, 320, 1024], P('fsdp', None, 'tp'), may hold values from -15 to 15
- connector: bfloat16 [8192, 6144], P('tp', 'fsdp'), may hold values from -0.75 to 0.75
- self_query: bfloat16 [8, 2, 1024, 3072], P('fsdp', None, 'tp'), may hold values from -15 to 15
- self_key: bfloat16 [8, 2, 1024, 3072], P('fsdp', None, 'tp'), may hold values from -15 to 15
- latent_value: bfloat16 [8, 2, 1024, 3072], P('fsdp', None, 'tp'), may hold values from -6 to 6
- cotangent: bfloat16 [8, 2, 1024, 3072], P('fsdp', None, 'tp'), may hold values from -6 to 6
Outputs:
- latent_out: bfloat16 [8, 2, 1024, 3072], P('fsdp', None, 'tp')
- self_grad: bfloat16 [8, 2, 1024, 3072], P('fsdp', None, 'tp')
- context_grad: bfloat16 [8, 2, 64, 3072], P('fsdp', None, None, 'tp')
The draws below stay inside these ranges and needn't reach their ends.
All inputs are finite; a program needn't handle non-finite values.
Results may differ from the reference program's by a relative error of at most 0.015.
Values may be sent and summed in bfloat16 or wider, within the bound.
A program may use at most 128 MiB of HBM per device.

```python
import jax
import jax.numpy as jnp
from jax import lax

HEAD_SIZE = 128
LLM_HEADS = 64
LLM_KV = 8
DENOISER_HEADS = 24
QUERY_TOKENS = 64
LATENT_TOKENS = 1024
SAMPLE_COUNT = 2
PROMPT = 256
LANGUAGE_WIDTH = 8192
DENOISER_WIDTH = 3072
PROMPT_COUNT = 8


def random_base(key, full_shape):
    return jnp.clip(jax.random.normal(key, full_shape, jnp.float32), -6.0, 6.0)


def draw_llm_query(key, part):
    final_output = random_base(jax.random.fold_in(key, 1), (PROMPT_COUNT, QUERY_TOKENS, LLM_HEADS * HEAD_SIZE))
    return final_output.astype(jnp.bfloat16)


def draw_llm_kv(key, part):
    final_output = random_base(jax.random.fold_in(key, 2), (PROMPT_COUNT, 2, PROMPT + QUERY_TOKENS, LLM_KV * HEAD_SIZE))
    return final_output.astype(jnp.bfloat16)


def draw_self_query(key, part):
    final_output = random_base(jax.random.fold_in(key, 3), (PROMPT_COUNT, SAMPLE_COUNT, LATENT_TOKENS, DENOISER_HEADS * HEAD_SIZE))
    return final_output.astype(jnp.bfloat16)


def draw_self_key(key, part):
    final_output = random_base(jax.random.fold_in(key, 4), (PROMPT_COUNT, SAMPLE_COUNT, LATENT_TOKENS, DENOISER_HEADS * HEAD_SIZE))
    return final_output.astype(jnp.bfloat16)


def block_levels(rng, extent, shards, low, high):
    factor_of = 1.0
    for position, blocks in shards:
        heights = jax.random.uniform(jax.random.fold_in(jax.random.fold_in(rng, 6), position), (blocks,), jnp.float32, low / len(shards), high / len(shards))
        factor_of = factor_of * jnp.repeat(jnp.exp(heights), extent[position] // blocks).reshape((-1,) + (1,) * (len(extent) - 1 - position))
    return factor_of


def noise(own_key, shape, width, reach, cuts=(), held_as=jnp.bfloat16):
    values = width * jax.random.normal(own_key, shape, jnp.float32)
    if cuts:
        values = values * block_levels(own_key, shape, cuts, -0.22, 0.18)
    return jnp.clip(values, -reach, reach).astype(held_as)


def setup_inputs(seed: int = 0) -> dict:
    arg_keys = jax.random.split(jax.random.key(seed), 8)
    llm_query = draw_llm_query(jax.random.fold_in(arg_keys[7], 71), 0)
    llm_kv = draw_llm_kv(jax.random.fold_in(arg_keys[7], 71), 0)
    connector = noise(arg_keys[2], (LANGUAGE_WIDTH, 2 * DENOISER_WIDTH), (LANGUAGE_WIDTH // 128) ** -0.5, 0.75, ((0, 4), (1, 8)))
    self_query = draw_self_query(jax.random.fold_in(arg_keys[7], 71), 0)
    self_key = draw_self_key(jax.random.fold_in(arg_keys[7], 71), 0)
    latent_value = noise(arg_keys[5], (PROMPT_COUNT, SAMPLE_COUNT, LATENT_TOKENS, DENOISER_WIDTH), 1.0, 6.0, ((0, 8), (2, 4)))
    cotangent = noise(arg_keys[6], (PROMPT_COUNT, SAMPLE_COUNT, LATENT_TOKENS, DENOISER_WIDTH), 1.0, 6.0, ((0, 8), (2, 4)))
    return dict(llm_query=llm_query, llm_kv=llm_kv, connector=connector, self_query=self_query, self_key=self_key, latent_value=latent_value, cotangent=cotangent)


norm_eps = 1e-06

def softmax_rows(scores, axis_index):
    top_value = lax.optimization_barrier(jnp.max(scores, axis=axis_index, keepdims=True))
    exp_terms = jnp.exp(scores - top_value)
    return exp_terms / lax.optimization_barrier(jnp.sum(exp_terms, axis=axis_index, keepdims=True))

def llm_attention(query_rows, key_value):
    group_size = LLM_HEADS // LLM_KV
    positions = PROMPT + QUERY_TOKENS
    queries = query_rows.reshape(QUERY_TOKENS, LLM_KV, group_size, HEAD_SIZE).astype(jnp.float32)
    keys_all = key_value[0].reshape(positions, LLM_KV, HEAD_SIZE).astype(jnp.float32)
    values_all = key_value[1].reshape(positions, LLM_KV, HEAD_SIZE).astype(jnp.float32)
    scores = jnp.einsum('qkgd,pkd->kgqp', queries, keys_all) * HEAD_SIZE ** (-0.5)
    allowed = jnp.arange(positions)[None, :] <= PROMPT + jnp.arange(QUERY_TOKENS)[:, None]
    scores = jnp.where(allowed, scores, -1e+30)
    weights = softmax_rows(scores, 3).astype(jnp.bfloat16)
    mixed_heads = jnp.einsum('kgqp,pkd->qkgd', weights.astype(jnp.float32), values_all)
    return mixed_heads.astype(jnp.bfloat16).reshape(QUERY_TOKENS, LLM_HEADS * HEAD_SIZE)

def self_item(operands):
    query_item, key_item, value_item = operands
    scores = jnp.dot(query_item, key_item.T, preferred_element_type=jnp.float32) * HEAD_SIZE ** (-0.5)
    weights = softmax_rows(scores, 1).astype(jnp.bfloat16)
    return jnp.dot(weights, value_item, preferred_element_type=jnp.float32).astype(jnp.bfloat16)

def rms_inverse(incoming_values):
    return lax.rsqrt(lax.optimization_barrier(jnp.mean(incoming_values * incoming_values, axis=-1, keepdims=True)) + norm_eps)

def norm_back(grad_normed, normed, inverse):
    return inverse * (grad_normed - normed * lax.optimization_barrier(jnp.mean(grad_normed * normed, axis=-1, keepdims=True)))

def cross_block(latent_heads, condition_tokens, gradient_heads):
    score_scale = HEAD_SIZE ** (-0.5)
    model_width = DENOISER_HEADS * HEAD_SIZE
    condition_keys = condition_tokens[:, :model_width].reshape(QUERY_TOKENS, DENOISER_HEADS, HEAD_SIZE)
    condition_values = condition_tokens[:, model_width:].reshape(QUERY_TOKENS, DENOISER_HEADS, HEAD_SIZE).astype(jnp.float32)
    self_float = latent_heads.astype(jnp.float32)
    query_inverse = rms_inverse(self_float)
    query_normed = self_float * query_inverse
    query_round = query_normed.astype(jnp.bfloat16).astype(jnp.float32)
    key_float = condition_keys.astype(jnp.float32)
    key_inverse = rms_inverse(key_float)
    key_normed = key_float * key_inverse
    key_round = key_normed.astype(jnp.bfloat16).astype(jnp.float32)
    scores = jnp.einsum('hrd,chd->hcr', query_round, key_round) * score_scale
    exp_terms = jnp.exp(scores)
    attention_weights = exp_terms / lax.optimization_barrier(jnp.sum(exp_terms, axis=1, keepdims=True))
    weights_round = attention_weights.astype(jnp.bfloat16).astype(jnp.float32)
    cross_out = jnp.einsum('hcr,chd->hrd', weights_round, condition_values)
    total_heads = self_float + cross_out
    grad_float = gradient_heads.astype(jnp.float32)
    value_gradient = jnp.einsum('hcr,hrd->chd', weights_round, grad_float)
    weight_grad = jnp.einsum('hrd,chd->hcr', grad_float, condition_values)
    delta_rows = lax.optimization_barrier(jnp.sum(attention_weights * weight_grad, axis=1, keepdims=True))
    score_grad = (attention_weights * (weight_grad - delta_rows) * score_scale).astype(jnp.bfloat16).astype(jnp.float32)
    query_grad = jnp.einsum('hcr,chd->hrd', score_grad, key_round)
    key_grad_normed = jnp.einsum('hcr,hrd->chd', score_grad, query_round)
    self_grad = grad_float + norm_back(query_grad, query_normed, query_inverse)
    key_gradient = norm_back(key_grad_normed, key_normed, key_inverse)
    return (total_heads, self_grad, key_gradient, value_gradient)

def one_prompt(connector, operands):
    query_rows, key_value, self_q, self_k, self_v, upstream_gradient = operands
    hidden = llm_attention(query_rows, key_value)
    condition_tokens = jnp.dot(hidden, connector, preferred_element_type=jnp.float32).astype(jnp.bfloat16)

    def to_items(incoming_values):
        return incoming_values.reshape(SAMPLE_COUNT, LATENT_TOKENS, DENOISER_HEADS, HEAD_SIZE).transpose(0, 2, 1, 3).reshape(SAMPLE_COUNT * DENOISER_HEADS, LATENT_TOKENS, HEAD_SIZE)
    latent_attention_output = lax.map(self_item, (to_items(self_q), to_items(self_k), to_items(self_v)))
    gathered_rows = SAMPLE_COUNT * LATENT_TOKENS
    latent_heads = latent_attention_output.reshape(SAMPLE_COUNT, DENOISER_HEADS, LATENT_TOKENS, HEAD_SIZE).transpose(1, 0, 2, 3).reshape(DENOISER_HEADS, gathered_rows, HEAD_SIZE)
    gradient_heads = upstream_gradient.reshape(SAMPLE_COUNT, LATENT_TOKENS, DENOISER_HEADS, HEAD_SIZE).transpose(2, 0, 1, 3).reshape(DENOISER_HEADS, gathered_rows, HEAD_SIZE)
    total_heads, self_grad, key_gradient, value_gradient = cross_block(latent_heads, condition_tokens, gradient_heads)

    def to_rows(incoming_values):
        return incoming_values.reshape(DENOISER_HEADS, SAMPLE_COUNT, LATENT_TOKENS, HEAD_SIZE).transpose(1, 2, 0, 3).reshape(SAMPLE_COUNT, LATENT_TOKENS, DENOISER_HEADS * HEAD_SIZE).astype(jnp.bfloat16)
    gradient_list = jnp.stack([key_gradient.reshape(QUERY_TOKENS, DENOISER_HEADS * HEAD_SIZE), value_gradient.reshape(QUERY_TOKENS, DENOISER_HEADS * HEAD_SIZE)])
    return (to_rows(total_heads), to_rows(self_grad), gradient_list.astype(jnp.bfloat16))

def reference(llm_query, llm_kv, connector, self_query, self_key, latent_value, cotangent):
    latent_out, self_grad, context_grad = lax.map(lambda operands: one_prompt(connector, operands), (llm_query, llm_kv, self_query, self_key, latent_value, cotangent))
    return (latent_out, self_grad, context_grad)
```

```python
import functools
import math

import jax
import jax.numpy as jnp
from jax import lax
from jax.experimental import pallas as pl
from jax.experimental.pallas import tpu as pltpu
from jax.sharding import PartitionSpec as P

HEAD_SIZE = 128
LLM_HEADS = 64
LLM_KV = 8
DENOISER_HEADS = 24
QUERY_TOKENS = 64
SAMPLE_COUNT = 2
PROMPT = 256
norm_eps = 1e-06
score_scale = HEAD_SIZE ** (-0.5)
NT = (((1,), (1,)), ((), ()))
TN = (((0,), (0,)), ((), ()))
NN = (((1,), (0,)), ((), ()))


def mm(a, b, dims):
    return lax.dot_general(a, b, dims, preferred_element_type=jnp.float32)


def exchange(value, mask):
    size = lax.axis_size("tp")
    return lax.ppermute(value, "tp", [(i, i ^ mask) for i in range(size)])


def tp_masks():
    size = lax.axis_size("tp")
    masks = []
    while size > 1:
        size //= 2
        masks.append(size)
    return masks


def reduce_scatter(blocks):
    masks = tp_masks()
    rest = blocks.shape[1:]
    blocks = blocks.reshape((2,) * len(masks) + rest)
    me = lax.axis_index("tp")
    for level in reversed(range(len(masks))):
        bit = (me // masks[level]) % 2
        kept = lax.dynamic_index_in_dim(blocks, bit, level, keepdims=False)
        sent = lax.dynamic_index_in_dim(blocks, 1 - bit, level, keepdims=False)
        came = exchange(sent.astype(jnp.bfloat16), masks[level])
        blocks = kept.astype(jnp.float32) + came.astype(jnp.float32)
    return blocks


def all_gather(block):
    me = lax.axis_index("tp")
    masks = tp_masks()
    rest = block.shape
    whole = block.reshape((1,) * len(masks) + rest)
    for level, mask in enumerate(masks):
        came = exchange(whole, mask)
        bit = (me // mask) % 2
        first = jnp.where(bit == 0, whole, came)
        second = jnp.where(bit == 0, came, whole)
        whole = jnp.concatenate([first, second], axis=level)
    return whole.reshape((-1,) + rest)


def llm_keys_values(llm_kv, kv_heads, first_kv_of):
    size = lax.axis_size("tp")
    me = lax.axis_index("tp")
    rows = llm_kv.shape[2]
    width = kv_heads * HEAD_SIZE
    local = llm_kv[0]
    whole = jnp.zeros((2, size, rows, width), llm_kv.dtype)
    for mask in range(size):
        other = me ^ mask
        part = lax.dynamic_slice_in_dim(local, first_kv_of(other) * HEAD_SIZE, width, 2)
        if mask:
            part = exchange(part, mask)
        whole = lax.dynamic_update_slice(whole, part[:, None], (0, other, 0, 0))
    return whole.reshape(2, size * rows, width)


def llm_hidden(llm_query, llm_kv):
    query_heads = llm_query.shape[2] // HEAD_SIZE
    group_total = LLM_HEADS // LLM_KV
    kv_heads = max(query_heads // group_total, 1)
    group_size = query_heads // kv_heads
    local_kv = llm_keys_values(llm_kv, kv_heads, lambda t: t * query_heads // group_total)
    positions = local_kv.shape[1]
    queries = llm_query[0].reshape(QUERY_TOKENS, kv_heads, group_size, HEAD_SIZE)
    keys_all = local_kv[0].reshape(positions, kv_heads, HEAD_SIZE)
    values_all = local_kv[1].reshape(positions, kv_heads, HEAD_SIZE)
    scores = (
        jnp.einsum("qkgd,pkd->kgqp", queries, keys_all, preferred_element_type=jnp.float32)
        * score_scale
    )
    allowed = jnp.arange(positions)[None, :] <= PROMPT + jnp.arange(QUERY_TOKENS)[:, None]
    scores = jnp.where(allowed, scores, -1e30)
    exp_terms = jnp.exp(scores - jnp.max(scores, axis=3, keepdims=True))
    weights = (exp_terms / jnp.sum(exp_terms, axis=3, keepdims=True)).astype(jnp.bfloat16)
    mixed_heads = jnp.einsum(
        "kgqp,pkd->qkgd", weights, values_all, preferred_element_type=jnp.float32
    )
    return mixed_heads.astype(jnp.bfloat16).reshape(QUERY_TOKENS, query_heads * HEAD_SIZE)


def context_of(llm_query, llm_kv, connector):
    hidden = llm_hidden(llm_query, llm_kv)
    every_hidden = lax.all_gather(hidden, "fsdp", axis=0, tiled=True)
    partial_kv = jnp.dot(every_hidden, connector, preferred_element_type=jnp.float32)
    size = lax.axis_size("tp")
    prompts = partial_kv.shape[0] // QUERY_TOKENS
    columns = partial_kv.shape[1]
    blocks = partial_kv.reshape(prompts, size, QUERY_TOKENS // size, columns)
    mine = reduce_scatter(blocks.transpose(1, 0, 2, 3)).astype(jnp.bfloat16)
    tokens = lax.all_to_all(mine, "fsdp", split_axis=0, concat_axis=2, tiled=True)[0]
    return all_gather(tokens).reshape(QUERY_TOKENS, -1)


def head_kernel(far, chained, *refs):
    q_ref, g_ref, ck_ref, cv_ref = refs[:4]
    refs = refs[4:]
    whole_keys, whole_values = refs[0:2], refs[2:4]
    far_refs = refs[4 : 4 + far]
    refs = refs[4 + far + (2 if chained else 0) :]
    out_ref, grad_ref, context_ref = refs
    rows = q_ref.shape[2]
    pieces = []
    for sample in range(SAMPLE_COUNT):
        query = q_ref[0, sample]
        keys = [r[0, sample] for r in whole_keys] + [r[0, sample] for r in far_refs]
        values = [r[0, sample] for r in whole_values] + [r[1, sample] for r in far_refs]
        scores = [mm(query, key, NT) for key in keys]
        top = functools.reduce(jnp.maximum, scores)
        top = jnp.max(top, axis=1, keepdims=True)
        terms = [jnp.exp((s - top) * score_scale) for s in scores]
        total = jnp.sum(functools.reduce(jnp.add, terms), axis=1, keepdims=True)
        mixed = functools.reduce(
            jnp.add, [mm(e.astype(jnp.bfloat16), v, NN) for e, v in zip(terms, values)]
        )
        pieces.append((mixed / total).astype(jnp.bfloat16))
    latent = jnp.concatenate(pieces, axis=0).astype(jnp.float32)
    inverse = lax.rsqrt(jnp.mean(latent * latent, axis=1, keepdims=True) + norm_eps)
    normed = latent * inverse
    query_round = normed.astype(jnp.bfloat16)
    key_float = ck_ref[...].astype(jnp.float32)
    key_inverse = lax.rsqrt(jnp.mean(key_float * key_float, axis=1, keepdims=True) + norm_eps)
    key_normed = key_float * key_inverse
    key_round = key_normed.astype(jnp.bfloat16)
    condition_values = cv_ref[...]
    gradient = g_ref[0].reshape(SAMPLE_COUNT * rows, HEAD_SIZE)
    exp_terms = jnp.exp(mm(key_round, query_round, NT) * score_scale)
    weights = exp_terms / jnp.sum(exp_terms, axis=0, keepdims=True)
    weights_round = weights.astype(jnp.bfloat16)
    out = latent + mm(weights_round, condition_values, TN)
    value_gradient = mm(weights_round, gradient, NN)
    weight_grad = mm(condition_values, gradient, NT)
    delta = jnp.sum(weights * weight_grad, axis=0, keepdims=True)
    score_grad = (weights * (weight_grad - delta) * score_scale).astype(jnp.bfloat16)
    query_grad = mm(score_grad, key_round, TN)
    key_grad = mm(score_grad, query_round, NN)
    grad = gradient.astype(jnp.float32) + inverse * (
        query_grad - normed * jnp.mean(query_grad * normed, axis=1, keepdims=True)
    )
    key_grad = key_inverse * (
        key_grad - key_normed * jnp.mean(key_grad * key_normed, axis=1, keepdims=True)
    )
    out_ref[0] = out.astype(jnp.bfloat16).reshape(SAMPLE_COUNT, rows, HEAD_SIZE)
    grad_ref[0] = grad.astype(jnp.bfloat16).reshape(SAMPLE_COUNT, rows, HEAD_SIZE)
    context_ref[0, 0] = key_grad.astype(jnp.bfloat16)
    context_ref[0, 1] = value_gradient.astype(jnp.bfloat16)


def attend(groups, start, taken, query, gradient, context, near, far, earlier):
    per_group = DENOISER_HEADS // groups
    rows = query.shape[2]

    def head(step):
        return step // taken * per_group + start + step % taken

    whole = pl.BlockSpec((1, SAMPLE_COUNT, rows, HEAD_SIZE), lambda i: (0, 0, 0, head(i)))
    chunk = pl.BlockSpec((2, SAMPLE_COUNT, rows, HEAD_SIZE), lambda i: (0, 0, 0, i))
    in_specs = [
        whole,
        whole,
        pl.BlockSpec((QUERY_TOKENS, HEAD_SIZE), lambda i: (0, head(i))),
        pl.BlockSpec((QUERY_TOKENS, HEAD_SIZE), lambda i: (0, DENOISER_HEADS + head(i))),
    ]
    in_specs += [whole] * len(near) + [chunk] * len(far)
    operands = [query, gradient, context, context, *near, *far]
    aliases = {}
    if earlier is not None:
        aliases = {len(operands): 0, len(operands) + 1: 1}
        operands += list(earlier)
        in_specs += [pl.BlockSpec(memory_space=pl.ANY)] * 2
    heads = groups * taken
    keys = query.shape[2] * (len(far) + 2)
    flops = heads * SAMPLE_COUNT * rows * HEAD_SIZE * (4 * keys + 12 * QUERY_TOKENS)
    return pl.pallas_call(
        functools.partial(head_kernel, len(far), earlier is not None),
        grid=(heads,),
        in_specs=in_specs,
        out_specs=[
            whole,
            whole,
            pl.BlockSpec(
                (1, 2, QUERY_TOKENS, HEAD_SIZE), lambda i: (i // taken, 0, 0, i % taken)
            ),
        ],
        out_shape=[
            jax.ShapeDtypeStruct(query.shape, jnp.bfloat16),
            jax.ShapeDtypeStruct(query.shape, jnp.bfloat16),
            jax.ShapeDtypeStruct((groups, 2, QUERY_TOKENS, taken * HEAD_SIZE), jnp.bfloat16),
        ],
        input_output_aliases=aliases,
        compiler_params=pltpu.CompilerParams(vmem_limit_bytes=40 * 1024 * 1024),
        cost_estimate=pl.CostEstimate(
            flops=4 * flops,
            bytes_accessed=heads * rows * HEAD_SIZE * 24,
            transcendentals=heads * SAMPLE_COUNT * rows * keys,
        ),
    )(*operands)


def head_pieces(per_group):
    pieces, start = [], 0
    while start < per_group:
        taken = max(1, (per_group - start) // 3)
        pieces.append((start, taken))
        start += taken
    return pieces


def shards(llm_query, llm_kv, connector, self_query, self_key, latent_value, cotangent):
    size = lax.axis_size("tp")
    groups = math.gcd(DENOISER_HEADS, size)
    masks = tp_masks()
    pieces = head_pieces(DENOISER_HEADS // groups)
    rows = self_query.shape[2]

    def piece_of(array, start, taken):
        array = array.reshape(SAMPLE_COUNT, rows, groups, -1, HEAD_SIZE)
        array = array[:, :, :, start : start + taken]
        return array.reshape(SAMPLE_COUNT, rows, groups * taken * HEAD_SIZE)

    far_parts = []
    for start, taken in pieces:
        parts = [
            jnp.stack([piece_of(self_key, start, taken), piece_of(latent_value, start, taken)])
        ]
        for mask in masks[:-1]:
            parts += [exchange(part, mask) for part in parts]
        far_parts.append(parts[1:])
    near = [
        self_key,
        exchange(self_key, masks[-1]),
        latent_value,
        exchange(latent_value, masks[-1]),
    ]
    context = context_of(llm_query, llm_kv, connector)
    earlier = None
    context_pieces = []
    for (start, taken), parts in zip(pieces, far_parts):
        far = parts + [exchange(part, masks[-1]) for part in parts]
        latent_out, self_grad, partial = attend(
            groups, start, taken, self_query, cotangent, context, near, far, earlier
        )
        earlier = (latent_out, self_grad)
        if groups == size:
            partial = reduce_scatter(partial).astype(jnp.bfloat16)
        context_pieces.append(partial)
    context_grad = jnp.concatenate(context_pieces, axis=-1)
    if groups == size:
        context_grad = context_grad[None]
    else:
        context_grad = context_grad.transpose(1, 2, 0, 3).reshape(1, 2, QUERY_TOKENS, -1)
        context_grad = lax.psum_scatter(context_grad, "tp", scatter_dimension=3, tiled=True)
    return (latent_out, self_grad, context_grad)


def solution(mesh):
    placed = (
        P("fsdp", None, "tp"),
        P("fsdp", None, "tp", None),
        P("tp", "fsdp"),
        P("fsdp", None, "tp", None),
        P("fsdp", None, "tp", None),
        P("fsdp", None, "tp", None),
        P("fsdp", None, "tp", None),
    )
    return jax.shard_map(
        shards,
        mesh=mesh,
        in_specs=placed,
        out_specs=(
            P("fsdp", None, "tp", None),
            P("fsdp", None, "tp", None),
            P("fsdp", None, None, "tp"),
        ),
        check_vma=False,
    )
```

```python
import functools
import math

import jax
import jax.numpy as jnp
from jax import lax
from jax.experimental import pallas as pl
from jax.experimental.pallas import tpu as pltpu
from jax.sharding import PartitionSpec as P

HEAD_SIZE = 128
LLM_HEADS = 64
LLM_KV = 8
DENOISER_HEADS = 24
QUERY_TOKENS = 64
SAMPLE_COUNT = 2
PROMPT = 256
norm_eps = 1e-06
score_scale = HEAD_SIZE ** (-0.5)
NT = (((1,), (1,)), ((), ()))
TN = (((0,), (0,)), ((), ()))
NN = (((1,), (0,)), ((), ()))


def mm(a, b, dims):
    return lax.dot_general(a, b, dims, preferred_element_type=jnp.float32)


def exchange(value, mask):
    size = lax.axis_size("tp")
    return lax.ppermute(value, "tp", [(i, i ^ mask) for i in range(size)])


def tp_masks():
    size = lax.axis_size("tp")
    masks = []
    while size > 1:
        size //= 2
        masks.append(size)
    return masks


def reduce_scatter(blocks):
    masks = tp_masks()
    rest = blocks.shape[1:]
    blocks = blocks.reshape((2,) * len(masks) + rest)
    me = lax.axis_index("tp")
    for level in reversed(range(len(masks))):
        bit = (me // masks[level]) % 2
        kept = lax.dynamic_index_in_dim(blocks, bit, level, keepdims=False)
        sent = lax.dynamic_index_in_dim(blocks, 1 - bit, level, keepdims=False)
        came = exchange(sent.astype(jnp.bfloat16), masks[level])
        blocks = kept.astype(jnp.float32) + came.astype(jnp.float32)
    return blocks


def all_gather(block):
    me = lax.axis_index("tp")
    masks = tp_masks()
    rest = block.shape
    whole = block.reshape((1,) * len(masks) + rest)
    for level, mask in enumerate(masks):
        came = exchange(whole, mask)
        bit = (me // mask) % 2
        first = jnp.where(bit == 0, whole, came)
        second = jnp.where(bit == 0, came, whole)
        whole = jnp.concatenate([first, second], axis=level)
    return whole.reshape((-1,) + rest)


def llm_keys_values(llm_kv, kv_heads, first_kv_of):
    size = lax.axis_size("tp")
    me = lax.axis_index("tp")
    rows = llm_kv.shape[2]
    width = kv_heads * HEAD_SIZE
    local = llm_kv[0]
    whole = jnp.zeros((2, size, rows, width), llm_kv.dtype)
    for mask in range(size):
        other = me ^ mask
        part = lax.dynamic_slice_in_dim(local, first_kv_of(other) * HEAD_SIZE, width, 2)
        if mask:
            part = exchange(part, mask)
        whole = lax.dynamic_update_slice(whole, part[:, None], (0, other, 0, 0))
    return whole.reshape(2, size * rows, width)


def llm_hidden(llm_query, llm_kv):
    query_heads = llm_query.shape[2] // HEAD_SIZE
    group_total = LLM_HEADS // LLM_KV
    kv_heads = max(query_heads // group_total, 1)
    group_size = query_heads // kv_heads
    local_kv = llm_keys_values(llm_kv, kv_heads, lambda t: t * query_heads // group_total)
    positions = local_kv.shape[1]
    queries = llm_query[0].reshape(QUERY_TOKENS, kv_heads, group_size, HEAD_SIZE)
    keys_all = local_kv[0].reshape(positions, kv_heads, HEAD_SIZE)
    values_all = local_kv[1].reshape(positions, kv_heads, HEAD_SIZE)
    scores = (
        jnp.einsum("qkgd,pkd->kgqp", queries, keys_all, preferred_element_type=jnp.float32)
        * score_scale
    )
    allowed = jnp.arange(positions)[None, :] <= PROMPT + jnp.arange(QUERY_TOKENS)[:, None]
    scores = jnp.where(allowed, scores, -1e30)
    exp_terms = jnp.exp(scores - jnp.max(scores, axis=3, keepdims=True))
    weights = (exp_terms / jnp.sum(exp_terms, axis=3, keepdims=True)).astype(jnp.bfloat16)
    mixed_heads = jnp.einsum(
        "kgqp,pkd->qkgd", weights, values_all, preferred_element_type=jnp.float32
    )
    return mixed_heads.astype(jnp.bfloat16).reshape(QUERY_TOKENS, query_heads * HEAD_SIZE)


def context_of(llm_query, llm_kv, connector):
    hidden = llm_hidden(llm_query, llm_kv)
    every_hidden = lax.all_gather(hidden, "fsdp", axis=0, tiled=True)
    partial_kv = jnp.dot(every_hidden, connector, preferred_element_type=jnp.float32)
    size = lax.axis_size("tp")
    prompts = partial_kv.shape[0] // QUERY_TOKENS
    columns = partial_kv.shape[1]
    blocks = partial_kv.reshape(prompts, size, QUERY_TOKENS // size, columns)
    mine = reduce_scatter(blocks.transpose(1, 0, 2, 3)).astype(jnp.bfloat16)
    tokens = lax.all_to_all(mine, "fsdp", split_axis=0, concat_axis=2, tiled=True)[0]
    return all_gather(tokens).reshape(QUERY_TOKENS, -1)


def head_kernel(far, chained, *refs):
    q_ref, g_ref, ck_ref, cv_ref = refs[:4]
    refs = refs[4:]
    whole_keys, whole_values = refs[0:2], refs[2:4]
    far_refs = refs[4 : 4 + far]
    refs = refs[4 + far + (2 if chained else 0) :]
    out_ref, grad_ref, context_ref = refs
    rows = q_ref.shape[2]
    pieces = []
    for sample in range(SAMPLE_COUNT):
        query = q_ref[0, sample]
        keys = [r[0, sample] for r in whole_keys] + [r[0, sample] for r in far_refs]
        values = [r[0, sample] for r in whole_values] + [r[1, sample] for r in far_refs]
        scores = [mm(query, key, NT) for key in keys]
        top = functools.reduce(jnp.maximum, scores)
        top = jnp.max(top, axis=1, keepdims=True)
        terms = [jnp.exp((s - top) * score_scale) for s in scores]
        total = jnp.sum(functools.reduce(jnp.add, terms), axis=1, keepdims=True)
        mixed = functools.reduce(
            jnp.add, [mm(e.astype(jnp.bfloat16), v, NN) for e, v in zip(terms, values)]
        )
        pieces.append((mixed / total).astype(jnp.bfloat16))
    latent = jnp.concatenate(pieces, axis=0).astype(jnp.float32)
    inverse = lax.rsqrt(jnp.mean(latent * latent, axis=1, keepdims=True) + norm_eps)
    normed = latent * inverse
    query_round = normed.astype(jnp.bfloat16)
    key_float = ck_ref[...].astype(jnp.float32)
    key_inverse = lax.rsqrt(jnp.mean(key_float * key_float, axis=1, keepdims=True) + norm_eps)
    key_normed = key_float * key_inverse
    key_round = key_normed.astype(jnp.bfloat16)
    condition_values = cv_ref[...]
    gradient = g_ref[0].reshape(SAMPLE_COUNT * rows, HEAD_SIZE)
    exp_terms = jnp.exp(mm(key_round, query_round, NT) * score_scale)
    weights = exp_terms / jnp.sum(exp_terms, axis=0, keepdims=True)
    weights_round = weights.astype(jnp.bfloat16)
    out = latent + mm(weights_round, condition_values, TN)
    value_gradient = mm(weights_round, gradient, NN)
    weight_grad = mm(condition_values, gradient, NT)
    delta = jnp.sum(weights * weight_grad, axis=0, keepdims=True)
    score_grad = (weights * (weight_grad - delta) * score_scale).astype(jnp.bfloat16)
    query_grad = mm(score_grad, key_round, TN)
    key_grad = mm(score_grad, query_round, NN)
    grad = gradient.astype(jnp.float32) + inverse * (
        query_grad - normed * jnp.mean(query_grad * normed, axis=1, keepdims=True)
    )
    key_grad = key_inverse * (
        key_grad - key_normed * jnp.mean(key_grad * key_normed, axis=1, keepdims=True)
    )
    out_ref[0] = out.astype(jnp.bfloat16).reshape(SAMPLE_COUNT, rows, HEAD_SIZE)
    grad_ref[0] = grad.astype(jnp.bfloat16).reshape(SAMPLE_COUNT, rows, HEAD_SIZE)
    context_ref[0, 0] = key_grad.astype(jnp.bfloat16)
    context_ref[0, 1] = value_gradient.astype(jnp.bfloat16)


def attend(groups, start, taken, query, gradient, context, near, far, earlier):
    per_group = DENOISER_HEADS // groups
    rows = query.shape[2]

    def head(step):
        return step // taken * per_group + start + step % taken

    whole = pl.BlockSpec((1, SAMPLE_COUNT, rows, HEAD_SIZE), lambda i: (0, 0, 0, head(i)))
    chunk = pl.BlockSpec((2, SAMPLE_COUNT, rows, HEAD_SIZE), lambda i: (0, 0, 0, i))
    in_specs = [
        whole,
        whole,
        pl.BlockSpec((QUERY_TOKENS, HEAD_SIZE), lambda i: (0, head(i))),
        pl.BlockSpec((QUERY_TOKENS, HEAD_SIZE), lambda i: (0, DENOISER_HEADS + head(i))),
    ]
    in_specs += [whole] * len(near) + [chunk] * len(far)
    operands = [query, gradient, context, context, *near, *far]
    aliases = {}
    if earlier is not None:
        aliases = {len(operands): 0, len(operands) + 1: 1}
        operands += list(earlier)
        in_specs += [pl.BlockSpec(memory_space=pl.ANY)] * 2
    heads = groups * taken
    keys = query.shape[2] * (len(far) + 2)
    flops = heads * SAMPLE_COUNT * rows * HEAD_SIZE * (4 * keys + 12 * QUERY_TOKENS)
    return pl.pallas_call(
        functools.partial(head_kernel, len(far), earlier is not None),
        grid=(heads,),
        in_specs=in_specs,
        out_specs=[
            whole,
            whole,
            pl.BlockSpec(
                (1, 2, QUERY_TOKENS, HEAD_SIZE), lambda i: (i // taken, 0, 0, i % taken)
            ),
        ],
        out_shape=[
            jax.ShapeDtypeStruct(query.shape, jnp.bfloat16),
            jax.ShapeDtypeStruct(query.shape, jnp.bfloat16),
            jax.ShapeDtypeStruct((groups, 2, QUERY_TOKENS, taken * HEAD_SIZE), jnp.bfloat16),
        ],
        input_output_aliases=aliases,
        compiler_params=pltpu.CompilerParams(vmem_limit_bytes=40 * 1024 * 1024),
        cost_estimate=pl.CostEstimate(
            flops=4 * flops,
            bytes_accessed=heads * rows * HEAD_SIZE * 24,
            transcendentals=heads * SAMPLE_COUNT * rows * keys,
        ),
    )(*operands)


def head_pieces(per_group):
    pieces, start = [], 0
    while start < per_group:
        taken = max(1, (per_group - start) // 3)
        pieces.append((start, taken))
        start += taken
    return pieces


MESH = pl.DeviceIdType.MESH
DEPTH = 3


def self_head(query_of, keys_of, values_of):
    pieces = []
    for sample in range(SAMPLE_COUNT):
        scores = [mm(query_of(sample), key, NT) for key in keys_of(sample)]
        top = jnp.max(functools.reduce(jnp.maximum, scores), axis=1, keepdims=True)
        terms = [jnp.exp((s - top) * score_scale) for s in scores]
        total = jnp.sum(functools.reduce(jnp.add, terms), axis=1, keepdims=True)
        mixed = functools.reduce(
            jnp.add, [mm(e.astype(jnp.bfloat16), v, NN) for e, v in zip(terms, values_of(sample))]
        )
        pieces.append((mixed / total).astype(jnp.bfloat16))
    return pieces


def cross_head(latent, context_keys, condition_values, gradient):
    latent = latent.astype(jnp.float32)
    inverse = lax.rsqrt(jnp.mean(latent * latent, axis=1, keepdims=True) + norm_eps)
    normed = latent * inverse
    query_round = normed.astype(jnp.bfloat16)
    key_float = context_keys.astype(jnp.float32)
    key_inverse = lax.rsqrt(jnp.mean(key_float * key_float, axis=1, keepdims=True) + norm_eps)
    key_normed = key_float * key_inverse
    key_round = key_normed.astype(jnp.bfloat16)
    exp_terms = jnp.exp(mm(key_round, query_round, NT) * score_scale)
    weights = exp_terms / jnp.sum(exp_terms, axis=0, keepdims=True)
    weights_round = weights.astype(jnp.bfloat16)
    out = latent + mm(weights_round, condition_values, TN)
    value_gradient = mm(weights_round, gradient, NN)
    weight_grad = mm(condition_values, gradient, NT)
    delta = jnp.sum(weights * weight_grad, axis=0, keepdims=True)
    score_grad = (weights * (weight_grad - delta) * score_scale).astype(jnp.bfloat16)
    query_grad = mm(score_grad, key_round, TN)
    key_grad = mm(score_grad, query_round, NN)
    grad = gradient.astype(jnp.float32) + inverse * (
        query_grad - normed * jnp.mean(query_grad * normed, axis=1, keepdims=True)
    )
    key_grad = key_inverse * (
        key_grad - key_normed * jnp.mean(key_grad * key_normed, axis=1, keepdims=True)
    )
    return tuple(a.astype(jnp.bfloat16) for a in (out, grad, key_grad, value_gradient))


def whole_kernel(
    size,
    prompts,
    llm_query_ref,
    llm_kv_ref,
    connector_ref,
    query_ref,
    key_ref,
    value_ref,
    cotangent_ref,
    out_ref,
    grad_ref,
    context_grad_ref,
    kv,
    q_all,
    g_all,
    latent,
    llm_q,
    llm_parts,
    connector,
    hidden,
    partial,
    sum_out,
    sum_in,
    half,
    half_out,
    half_in,
    mine,
    context,
    pg,
    pg_near,
    pg_out,
    pg_far,
    load_sem,
    whole_sem,
    far_send,
    far_recv,
    near_send,
    near_recv,
    pass_send,
    pass_recv,
    llm_send,
    llm_recv,
    hidden_send,
    hidden_recv,
    sum_send,
    sum_recv,
    token_send,
    token_recv,
    gather_send,
    gather_recv,
    pg_send,
    pg_recv,
    out_sem,
):
    me = lax.axis_index("tp")
    row = lax.axis_index("fsdp")
    core = me % 2
    half_index = me // 2
    near = me + 1 - 2 * core
    far = me + 2 - 4 * half_index
    heads = DENOISER_HEADS
    per = heads // size
    rows = query_ref.shape[2]
    block = QUERY_TOKENS // size
    llm_width = llm_parts.shape[3]
    columns = connector_ref.shape[1]
    bf = jnp.bfloat16

    def peer_at(distance):
        low, high = distance % 2, distance // 2
        new_core = core + low - 2 * core * low
        new_half = half_index + high - 2 * half_index * high
        return new_half * 2 + new_core

    def remote(src, dst, send, recv, **where):
        return pltpu.make_async_remote_copy(
            src_ref=src,
            dst_ref=dst,
            send_sem=send,
            recv_sem=recv,
            device_id=where,
            device_id_type=MESH,
        )

    def head_of(i):
        return (i % size) * per + i // size

    def cols(i):
        return pl.ds(pl.multiple_of(head_of(i) * HEAD_SIZE, HEAD_SIZE), HEAD_SIZE)

    def load(i, which):
        source = (key_ref, value_ref)[which]
        return pltpu.make_async_copy(
            source.at[0, :, :, cols(i)], kv.at[0, i, which], load_sem.at[i, which]
        )

    def far_copy(i):
        return remote(kv.at[0, i], kv.at[2, i], far_send.at[i], far_recv.at[i], tp=far)

    def near_copy(i):
        return remote(kv.at[0, i], kv.at[1, i], near_send.at[i], near_recv.at[i], tp=near)

    def pass_copy(i):
        return remote(kv.at[2, i], kv.at[3, i], pass_send.at[i], pass_recv.at[i], tp=near)

    def llm_copy(d):
        start = pl.multiple_of(peer_at(d) * llm_width, HEAD_SIZE)
        return remote(
            llm_kv_ref.at[0, :, :, pl.ds(start, llm_width)],
            llm_parts.at[me],
            llm_send.at[d - 1],
            llm_recv.at[d - 1],
            tp=peer_at(d),
        )

    def llm_came(d):
        there = llm_parts.at[peer_at(d)]
        return remote(there, there, llm_send.at[d - 1], llm_recv.at[d - 1], tp=peer_at(d))

    own_start = pl.multiple_of(me * llm_width, HEAD_SIZE)
    llm_q_load = pltpu.make_async_copy(llm_query_ref.at[0], llm_q, whole_sem.at[0])
    llm_own_load = pltpu.make_async_copy(
        llm_kv_ref.at[0, :, :, pl.ds(own_start, llm_width)], llm_parts.at[me], whole_sem.at[1]
    )
    q_load = pltpu.make_async_copy(query_ref.at[0], q_all, whole_sem.at[2])
    g_load = pltpu.make_async_copy(cotangent_ref.at[0], g_all, whole_sem.at[3])
    connector_load = pltpu.make_async_copy(connector_ref, connector, whole_sem.at[4])

    llm_q_load.start()
    llm_own_load.start()

    @pl.loop(0, heads)
    def _(i):
        load(i, 0).start()
        load(i, 1).start()

    q_load.start()
    connector_load.start()
    g_load.start()

    barrier = pltpu.get_barrier_semaphore()
    for d in range(1, size):
        pl.semaphore_signal(barrier, inc=1, device_id={"tp": peer_at(d)}, device_id_type=MESH)
    for d in range(1, prompts):
        pl.semaphore_signal(
            barrier, inc=1, device_id={"fsdp": (row + d) % prompts}, device_id_type=MESH
        )
    pl.semaphore_wait(barrier, size - 1 + prompts - 1)

    for d in range(size - 1, 0, -1):
        llm_copy(d).start()

    @pl.loop(0, DEPTH)
    def _(i):
        load(i, 0).wait()
        load(i, 1).wait()
        far_copy(i).start()
        near_copy(i).start()

    @pl.loop(DEPTH, heads)
    def _(i):
        load(i, 0).wait()
        load(i, 1).wait()
        near_copy(i).start()

    llm_q_load.wait()
    llm_own_load.wait()
    for d in range(1, size):
        llm_came(d).wait_recv()
    kv_heads = llm_width // HEAD_SIZE
    group = llm_q.shape[1] // llm_width
    positions = size * llm_parts.shape[2]
    shape = (group * QUERY_TOKENS, positions)
    token = lax.broadcasted_iota(jnp.int32, shape, 0) % QUERY_TOKENS
    allowed = lax.broadcasted_iota(jnp.int32, shape, 1) <= PROMPT + token
    for k in range(kv_heads):
        at = slice(k * HEAD_SIZE, (k + 1) * HEAD_SIZE)
        base = k * group * HEAD_SIZE
        stacked = jnp.concatenate(
            [llm_q[:, base + j * HEAD_SIZE : base + (j + 1) * HEAD_SIZE] for j in range(group)], 0
        )
        keys = jnp.concatenate([llm_parts[j, 0, :, at] for j in range(size)], 0)
        values = jnp.concatenate([llm_parts[j, 1, :, at] for j in range(size)], 0)
        scores = jnp.where(allowed, mm(stacked, keys, NT) * score_scale, -1e30)
        terms = jnp.exp(scores - jnp.max(scores, axis=1, keepdims=True))
        total = jnp.sum(terms, axis=1, keepdims=True)
        mixed = (mm((terms / total).astype(bf), values, NN)).astype(bf)
        for j in range(group):
            hidden[row, :, base + j * HEAD_SIZE : base + (j + 1) * HEAD_SIZE] = mixed[
                j * QUERY_TOKENS : (j + 1) * QUERY_TOKENS
            ]

    def hidden_copy(d):
        return remote(
            hidden.at[row],
            hidden.at[row],
            hidden_send.at[d - 1],
            hidden_recv.at[d - 1],
            fsdp=(row + d) % prompts,
        )

    def hidden_came(d):
        there = hidden.at[(row + prompts - d) % prompts]
        return remote(
            there,
            there,
            hidden_send.at[d - 1],
            hidden_recv.at[d - 1],
            fsdp=(row + d) % prompts,
        )

    for d in range(1, prompts):
        hidden_copy(d).start()

    sum_copy = remote(sum_out, sum_in, sum_send.at[0], sum_recv.at[0], tp=near)
    half_copy = remote(half_out, half_in, sum_send.at[1], sum_recv.at[1], tp=far)

    def project():
        for d in range(1, prompts):
            hidden_came(d).wait_recv()
        connector_load.wait()
        rows_in = hidden[...].reshape(prompts * QUERY_TOKENS, hidden.shape[2])
        tile = HEAD_SIZE

        @pl.loop(0, columns // tile)
        def _(c):
            at = pl.ds(pl.multiple_of(c * tile, tile), tile)
            product = mm(rows_in, connector[:, at], NN)
            partial[:, :, :, at] = product.reshape(prompts, size, block, tile)

        for h in range(2):
            sum_out[h] = partial[:, 2 * h + 1 - core].astype(bf)
        sum_copy.start()

    def halve():
        sum_copy.wait_recv()
        half[...] = partial[:, 2 * half_index + core] + sum_in[half_index].astype(jnp.float32)
        other = 1 - half_index
        half_out[...] = (partial[:, 2 * other + core] + sum_in[other].astype(jnp.float32)).astype(bf)
        half_copy.start()

    def token_copy(d):
        to = (row + d) % prompts
        return remote(
            mine.at[to], context.at[me, row], token_send.at[d - 1], token_recv.at[d - 1], fsdp=to
        )

    def token_came(d):
        there = context.at[me, (row + prompts - d) % prompts]
        return remote(
            there,
            there,
            token_send.at[d - 1],
            token_recv.at[d - 1],
            fsdp=(row + d) % prompts,
        )

    def spread():
        half_copy.wait_recv()
        mine[...] = (half[...] + half_in[...].astype(jnp.float32)).astype(bf)
        context[me, row] = mine[row]
        for d in range(1, prompts):
            token_copy(d).start()

    def gather_copy(k, who, to):
        return remote(context.at[who], context.at[who], gather_send.at[k], gather_recv.at[k], tp=to)

    def gather_far():
        for d in range(1, prompts):
            token_came(d).wait_recv()
        gather_copy(0, me, far).start()
        gather_copy(1, me, near).start()

    def gather_near():
        gather_copy(0, far, far).wait_recv()
        gather_copy(2, far, near).start()

    def gathered():
        gather_copy(1, near, near).wait_recv()
        gather_copy(2, peer_at(3), near).wait_recv()
        g_load.wait()

    def condition(position):
        at = pl.ds(pl.multiple_of(position % columns, HEAD_SIZE), HEAD_SIZE)
        return context[:, position // columns, :, at].reshape(QUERY_TOKENS, HEAD_SIZE)

    def out_copy(i, which):
        if which == 0:
            source, target = latent.at[i], out_ref
        else:
            source, target = g_all.at[:, :, cols(i)], grad_ref
        return pltpu.make_async_copy(source, target.at[0, :, :, cols(i)], out_sem.at[i, which])

    def cross(i):
        start = head_of(i) * HEAD_SIZE
        out, grad, key_grad, value_gradient = cross_head(
            latent[i].reshape(SAMPLE_COUNT * rows, HEAD_SIZE),
            condition(start),
            condition(heads * HEAD_SIZE + start),
            g_all[:, :, cols(i)].reshape(SAMPLE_COUNT * rows, HEAD_SIZE),
        )
        latent[i] = out.reshape(SAMPLE_COUNT, rows, HEAD_SIZE)
        g_all[:, :, cols(i)] = grad.reshape(SAMPLE_COUNT, rows, HEAD_SIZE)
        out_copy(i, 0).start()
        out_copy(i, 1).start()
        pg[i % size, i // size, 0] = key_grad
        pg[i % size, i // size, 1] = value_gradient

    batches = ((0, per - 1), (per - 1, 1))

    def pg_near_copy(b, h):
        at = pl.ds(*batches[b])
        return remote(
            pg.at[2 * h + 1 - core, at],
            pg_near.at[h, at],
            pg_send.at[3 * b + h],
            pg_recv.at[3 * b + h],
            tp=near,
        )

    def pg_far_copy(b):
        at = pl.ds(*batches[b])
        return remote(
            pg_out.at[at], pg_far.at[at], pg_send.at[3 * b + 2], pg_recv.at[3 * b + 2], tp=far
        )

    def pg_start(b):
        for h in range(2):
            pg_near_copy(b, h).start()

    def pg_middle(b):
        for h in range(2):
            pg_near_copy(b, h).wait_recv()
        at = pl.ds(*batches[b])
        other = 1 - half_index
        total = pg[2 * other + core, at].astype(jnp.float32) + pg_near[other, at].astype(jnp.float32)
        pg_out[at] = total.astype(bf)
        pg_far_copy(b).start()

    def pg_end(b):
        pg_far_copy(b).wait_recv()
        first, count = batches[b]
        for s in range(first, first + count):
            total = (
                pg[me, s].astype(jnp.float32)
                + pg_near[half_index, s].astype(jnp.float32)
                + pg_far[s].astype(jnp.float32)
            )
            context_grad_ref[0, :, :, s * HEAD_SIZE : (s + 1) * HEAD_SIZE] = total.astype(bf)

    q_load.wait()
    ready = heads * 15 // 24

    @pl.loop(0, heads)
    def _(i):
        far_copy(i).wait_recv()
        pass_copy(i).start()

        @pl.when(i + DEPTH < heads)
        def _():
            far_copy(i + DEPTH).start()

        near_copy(i).wait_recv()
        for at, work in (
            (heads * 4 // 24, project),
            (heads * 5 // 24, halve),
            (heads * 9 // 24, spread),
            (heads * 10 // 24, gather_far),
            (heads * 14 // 24, gather_near),
            (ready, gathered),
            (heads * 22 // 24, functools.partial(pg_middle, 0)),
        ):
            pl.when(i == at)(work)
        pass_copy(i).wait_recv()

        def part(which):
            def of(sample):
                return [kv[source, i, which, sample] for source in range(size)]

            return of

        pieces = self_head(lambda sample: q_all[sample, :, cols(i)], part(0), part(1))
        for sample in range(SAMPLE_COUNT):
            latent[i, sample] = pieces[sample]

        first = jnp.where(i < ready, i + 1, jnp.where(i == ready, 0, i))

        @pl.loop(first, i + 1)
        def _(c):
            cross(c)

        @pl.when(i == size * (per - 1) - 1)
        def _():
            pg_start(0)

    pg_start(1)
    pg_end(0)
    pg_middle(1)
    pg_end(1)

    @pl.loop(0, heads)
    def _(i):
        far_copy(i).wait_send()
        near_copy(i).wait_send()
        pass_copy(i).wait_send()
        out_copy(i, 0).wait()
        out_copy(i, 1).wait()

    for d in range(1, size):
        llm_copy(d).wait_send()
    for d in range(1, prompts):
        hidden_copy(d).wait_send()
        token_copy(d).wait_send()
    sum_copy.wait_send()
    half_copy.wait_send()
    gather_copy(0, me, far).wait_send()
    gather_copy(1, me, near).wait_send()
    gather_copy(2, far, near).wait_send()
    for b in range(2):
        for h in range(2):
            pg_near_copy(b, h).wait_send()
        pg_far_copy(b).wait_send()


def whole_call(arrays):
    llm_query, llm_kv, connector, self_query, self_key, latent_value, cotangent = arrays
    size = lax.axis_size("tp")
    prompts = lax.axis_size("fsdp")
    heads = DENOISER_HEADS
    per = heads // size
    rows = self_query.shape[2]
    block = QUERY_TOKENS // size
    columns = connector.shape[1]
    llm_width = llm_query.shape[2] // (LLM_HEADS // LLM_KV)
    bf = jnp.bfloat16
    dma = pltpu.SemaphoreType.DMA
    width = heads * HEAD_SIZE
    any_space = pl.BlockSpec(memory_space=pl.ANY)
    token_block = (prompts, block, columns)
    return pl.pallas_call(
        functools.partial(whole_kernel, size, prompts),
        in_specs=[any_space] * 7,
        out_specs=[any_space, any_space, pl.BlockSpec(memory_space=pltpu.VMEM)],
        out_shape=[
            jax.ShapeDtypeStruct(self_query.shape, bf),
            jax.ShapeDtypeStruct(self_query.shape, bf),
            jax.ShapeDtypeStruct((1, 2, QUERY_TOKENS, per * HEAD_SIZE), bf),
        ],
        scratch_shapes=[
            pltpu.VMEM((size, heads, 2, SAMPLE_COUNT, rows, HEAD_SIZE), bf),
            pltpu.VMEM((SAMPLE_COUNT, rows, width), bf),
            pltpu.VMEM((SAMPLE_COUNT, rows, width), bf),
            pltpu.VMEM((heads, SAMPLE_COUNT, rows, HEAD_SIZE), bf),
            pltpu.VMEM(llm_query.shape[1:], bf),
            pltpu.VMEM((size, 2, llm_kv.shape[2], llm_width), bf),
            pltpu.VMEM(connector.shape, bf),
            pltpu.VMEM((prompts, QUERY_TOKENS, llm_query.shape[2]), bf),
            pltpu.VMEM((prompts, size, block, columns), jnp.float32),
            pltpu.VMEM((2,) + token_block, bf),
            pltpu.VMEM((2,) + token_block, bf),
            pltpu.VMEM(token_block, jnp.float32),
            pltpu.VMEM(token_block, bf),
            pltpu.VMEM(token_block, bf),
            pltpu.VMEM(token_block, bf),
            pltpu.VMEM((size,) + token_block, bf),
            pltpu.VMEM((size, per, 2, QUERY_TOKENS, HEAD_SIZE), bf),
            pltpu.VMEM((2, per, 2, QUERY_TOKENS, HEAD_SIZE), bf),
            pltpu.VMEM((per, 2, QUERY_TOKENS, HEAD_SIZE), bf),
            pltpu.VMEM((per, 2, QUERY_TOKENS, HEAD_SIZE), bf),
            dma((heads, 2)),
            dma((5,)),
            dma((heads,)),
            dma((heads,)),
            dma((heads,)),
            dma((heads,)),
            dma((heads,)),
            dma((heads,)),
            dma((size - 1,)),
            dma((size - 1,)),
            dma((prompts - 1,)),
            dma((prompts - 1,)),
            dma((2,)),
            dma((2,)),
            dma((prompts - 1,)),
            dma((prompts - 1,)),
            dma((3,)),
            dma((3,)),
            dma((6,)),
            dma((6,)),
            dma((heads, 2)),
        ],
        compiler_params=pltpu.CompilerParams(
            collective_id=0, has_side_effects=True, vmem_limit_bytes=60 * 1024 * 1024
        ),
        cost_estimate=pl.CostEstimate(
            flops=10**10, bytes_accessed=23 * 10**6, transcendentals=10**7
        ),
    )(*arrays)


def one_kernel_fits(connector):
    size = lax.axis_size("tp")
    return (
        len(tp_masks()) == 2
        and DENOISER_HEADS % size == 0
        and LLM_KV % size == 0
        and QUERY_TOKENS % (16 * size) == 0
        and connector.shape[1] % HEAD_SIZE == 0
    )


def shards(llm_query, llm_kv, connector, self_query, self_key, latent_value, cotangent):
    if one_kernel_fits(connector):
        return whole_call(
            (llm_query, llm_kv, connector, self_query, self_key, latent_value, cotangent)
        )
    size = lax.axis_size("tp")
    groups = math.gcd(DENOISER_HEADS, size)
    masks = tp_masks()
    pieces = head_pieces(DENOISER_HEADS // groups)
    rows = self_query.shape[2]

    def piece_of(array, start, taken):
        array = array.reshape(SAMPLE_COUNT, rows, groups, -1, HEAD_SIZE)
        array = array[:, :, :, start : start + taken]
        return array.reshape(SAMPLE_COUNT, rows, groups * taken * HEAD_SIZE)

    far_parts = []
    for start, taken in pieces:
        parts = [
            jnp.stack([piece_of(self_key, start, taken), piece_of(latent_value, start, taken)])
        ]
        for mask in masks[:-1]:
            parts += [exchange(part, mask) for part in parts]
        far_parts.append(parts[1:])
    near = [
        self_key,
        exchange(self_key, masks[-1]),
        latent_value,
        exchange(latent_value, masks[-1]),
    ]
    context = context_of(llm_query, llm_kv, connector)
    earlier = None
    context_pieces = []
    for (start, taken), parts in zip(pieces, far_parts):
        far = parts + [exchange(part, masks[-1]) for part in parts]
        latent_out, self_grad, partial = attend(
            groups, start, taken, self_query, cotangent, context, near, far, earlier
        )
        earlier = (latent_out, self_grad)
        if groups == size:
            partial = reduce_scatter(partial).astype(jnp.bfloat16)
        context_pieces.append(partial)
    context_grad = jnp.concatenate(context_pieces, axis=-1)
    if groups == size:
        context_grad = context_grad[None]
    else:
        context_grad = context_grad.transpose(1, 2, 0, 3).reshape(1, 2, QUERY_TOKENS, -1)
        context_grad = lax.psum_scatter(context_grad, "tp", scatter_dimension=3, tiled=True)
    return (latent_out, self_grad, context_grad)


def solution(mesh):
    placed = (
        P("fsdp", None, "tp"),
        P("fsdp", None, "tp", None),
        P("tp", "fsdp"),
        P("fsdp", None, "tp", None),
        P("fsdp", None, "tp", None),
        P("fsdp", None, "tp", None),
        P("fsdp", None, "tp", None),
    )
    return jax.shard_map(
        shards,
        mesh=mesh,
        in_specs=placed,
        out_specs=(
            P("fsdp", None, "tp", None),
            P("fsdp", None, "tp", None),
            P("fsdp", None, None, "tp"),
        ),
        check_vma=False,
    )
```

```python
import functools
import math

import jax
import jax.numpy as jnp
from jax import lax
from jax.experimental import pallas as pl
from jax.experimental.pallas import tpu as pltpu
from jax.sharding import PartitionSpec as P

HEAD_SIZE = 128
LLM_HEADS = 64
LLM_KV = 8
DENOISER_HEADS = 24
QUERY_TOKENS = 64
SAMPLE_COUNT = 2
PROMPT = 256
norm_eps = 1e-06
score_scale = HEAD_SIZE ** (-0.5)
NT = (((1,), (1,)), ((), ()))
TN = (((0,), (0,)), ((), ()))
NN = (((1,), (0,)), ((), ()))


def mm(a, b, dims):
    return lax.dot_general(a, b, dims, preferred_element_type=jnp.float32)


def exchange(value, mask):
    size = lax.axis_size("tp")
    return lax.ppermute(value, "tp", [(i, i ^ mask) for i in range(size)])


def tp_masks():
    size = lax.axis_size("tp")
    masks = []
    while size > 1:
        size //= 2
        masks.append(size)
    return masks


def reduce_scatter(blocks):
    masks = tp_masks()
    rest = blocks.shape[1:]
    blocks = blocks.reshape((2,) * len(masks) + rest)
    me = lax.axis_index("tp")
    for level in reversed(range(len(masks))):
        bit = (me // masks[level]) % 2
        kept = lax.dynamic_index_in_dim(blocks, bit, level, keepdims=False)
        sent = lax.dynamic_index_in_dim(blocks, 1 - bit, level, keepdims=False)
        came = exchange(sent.astype(jnp.bfloat16), masks[level])
        blocks = kept.astype(jnp.float32) + came.astype(jnp.float32)
    return blocks


def all_gather(block):
    me = lax.axis_index("tp")
    masks = tp_masks()
    rest = block.shape
    whole = block.reshape((1,) * len(masks) + rest)
    for level, mask in enumerate(masks):
        came = exchange(whole, mask)
        bit = (me // mask) % 2
        first = jnp.where(bit == 0, whole, came)
        second = jnp.where(bit == 0, came, whole)
        whole = jnp.concatenate([first, second], axis=level)
    return whole.reshape((-1,) + rest)


def llm_keys_values(llm_kv, kv_heads, first_kv_of):
    size = lax.axis_size("tp")
    me = lax.axis_index("tp")
    rows = llm_kv.shape[2]
    width = kv_heads * HEAD_SIZE
    local = llm_kv[0]
    whole = jnp.zeros((2, size, rows, width), llm_kv.dtype)
    for mask in range(size):
        other = me ^ mask
        part = lax.dynamic_slice_in_dim(local, first_kv_of(other) * HEAD_SIZE, width, 2)
        if mask:
            part = exchange(part, mask)
        whole = lax.dynamic_update_slice(whole, part[:, None], (0, other, 0, 0))
    return whole.reshape(2, size * rows, width)


def llm_hidden(llm_query, llm_kv):
    query_heads = llm_query.shape[2] // HEAD_SIZE
    group_total = LLM_HEADS // LLM_KV
    kv_heads = max(query_heads // group_total, 1)
    group_size = query_heads // kv_heads
    local_kv = llm_keys_values(llm_kv, kv_heads, lambda t: t * query_heads // group_total)
    positions = local_kv.shape[1]
    queries = llm_query[0].reshape(QUERY_TOKENS, kv_heads, group_size, HEAD_SIZE)
    keys_all = local_kv[0].reshape(positions, kv_heads, HEAD_SIZE)
    values_all = local_kv[1].reshape(positions, kv_heads, HEAD_SIZE)
    scores = (
        jnp.einsum("qkgd,pkd->kgqp", queries, keys_all, preferred_element_type=jnp.float32)
        * score_scale
    )
    allowed = jnp.arange(positions)[None, :] <= PROMPT + jnp.arange(QUERY_TOKENS)[:, None]
    scores = jnp.where(allowed, scores, -1e30)
    exp_terms = jnp.exp(scores - jnp.max(scores, axis=3, keepdims=True))
    weights = (exp_terms / jnp.sum(exp_terms, axis=3, keepdims=True)).astype(jnp.bfloat16)
    mixed_heads = jnp.einsum(
        "kgqp,pkd->qkgd", weights, values_all, preferred_element_type=jnp.float32
    )
    return mixed_heads.astype(jnp.bfloat16).reshape(QUERY_TOKENS, query_heads * HEAD_SIZE)


def context_of(llm_query, llm_kv, connector):
    hidden = llm_hidden(llm_query, llm_kv)
    every_hidden = lax.all_gather(hidden, "fsdp", axis=0, tiled=True)
    partial_kv = jnp.dot(every_hidden, connector, preferred_element_type=jnp.float32)
    size = lax.axis_size("tp")
    prompts = partial_kv.shape[0] // QUERY_TOKENS
    columns = partial_kv.shape[1]
    blocks = partial_kv.reshape(prompts, size, QUERY_TOKENS // size, columns)
    mine = reduce_scatter(blocks.transpose(1, 0, 2, 3)).astype(jnp.bfloat16)
    tokens = lax.all_to_all(mine, "fsdp", split_axis=0, concat_axis=2, tiled=True)[0]
    return all_gather(tokens).reshape(QUERY_TOKENS, -1)


def head_kernel(far, chained, *refs):
    q_ref, g_ref, ck_ref, cv_ref = refs[:4]
    refs = refs[4:]
    whole_keys, whole_values = refs[0:2], refs[2:4]
    far_refs = refs[4 : 4 + far]
    refs = refs[4 + far + (2 if chained else 0) :]
    out_ref, grad_ref, context_ref = refs
    rows = q_ref.shape[2]
    pieces = []
    for sample in range(SAMPLE_COUNT):
        query = q_ref[0, sample]
        keys = [r[0, sample] for r in whole_keys] + [r[0, sample] for r in far_refs]
        values = [r[0, sample] for r in whole_values] + [r[1, sample] for r in far_refs]
        scores = [mm(query, key, NT) for key in keys]
        top = functools.reduce(jnp.maximum, scores)
        top = jnp.max(top, axis=1, keepdims=True)
        terms = [jnp.exp((s - top) * score_scale) for s in scores]
        total = jnp.sum(functools.reduce(jnp.add, terms), axis=1, keepdims=True)
        mixed = functools.reduce(
            jnp.add, [mm(e.astype(jnp.bfloat16), v, NN) for e, v in zip(terms, values)]
        )
        pieces.append((mixed / total).astype(jnp.bfloat16))
    latent = jnp.concatenate(pieces, axis=0).astype(jnp.float32)
    inverse = lax.rsqrt(jnp.mean(latent * latent, axis=1, keepdims=True) + norm_eps)
    normed = latent * inverse
    query_round = normed.astype(jnp.bfloat16)
    key_float = ck_ref[...].astype(jnp.float32)
    key_inverse = lax.rsqrt(jnp.mean(key_float * key_float, axis=1, keepdims=True) + norm_eps)
    key_normed = key_float * key_inverse
    key_round = key_normed.astype(jnp.bfloat16)
    condition_values = cv_ref[...]
    gradient = g_ref[0].reshape(SAMPLE_COUNT * rows, HEAD_SIZE)
    exp_terms = jnp.exp(mm(key_round, query_round, NT) * score_scale)
    weights = exp_terms / jnp.sum(exp_terms, axis=0, keepdims=True)
    weights_round = weights.astype(jnp.bfloat16)
    out = latent + mm(weights_round, condition_values, TN)
    value_gradient = mm(weights_round, gradient, NN)
    weight_grad = mm(condition_values, gradient, NT)
    delta = jnp.sum(weights * weight_grad, axis=0, keepdims=True)
    score_grad = (weights * (weight_grad - delta) * score_scale).astype(jnp.bfloat16)
    query_grad = mm(score_grad, key_round, TN)
    key_grad = mm(score_grad, query_round, NN)
    grad = gradient.astype(jnp.float32) + inverse * (
        query_grad - normed * jnp.mean(query_grad * normed, axis=1, keepdims=True)
    )
    key_grad = key_inverse * (
        key_grad - key_normed * jnp.mean(key_grad * key_normed, axis=1, keepdims=True)
    )
    out_ref[0] = out.astype(jnp.bfloat16).reshape(SAMPLE_COUNT, rows, HEAD_SIZE)
    grad_ref[0] = grad.astype(jnp.bfloat16).reshape(SAMPLE_COUNT, rows, HEAD_SIZE)
    context_ref[0, 0] = key_grad.astype(jnp.bfloat16)
    context_ref[0, 1] = value_gradient.astype(jnp.bfloat16)


def attend(groups, start, taken, query, gradient, context, near, far, earlier):
    per_group = DENOISER_HEADS // groups
    rows = query.shape[2]

    def head(step):
        return step // taken * per_group + start + step % taken

    whole = pl.BlockSpec((1, SAMPLE_COUNT, rows, HEAD_SIZE), lambda i: (0, 0, 0, head(i)))
    chunk = pl.BlockSpec((2, SAMPLE_COUNT, rows, HEAD_SIZE), lambda i: (0, 0, 0, i))
    in_specs = [
        whole,
        whole,
        pl.BlockSpec((QUERY_TOKENS, HEAD_SIZE), lambda i: (0, head(i))),
        pl.BlockSpec((QUERY_TOKENS, HEAD_SIZE), lambda i: (0, DENOISER_HEADS + head(i))),
    ]
    in_specs += [whole] * len(near) + [chunk] * len(far)
    operands = [query, gradient, context, context, *near, *far]
    aliases = {}
    if earlier is not None:
        aliases = {len(operands): 0, len(operands) + 1: 1}
        operands += list(earlier)
        in_specs += [pl.BlockSpec(memory_space=pl.ANY)] * 2
    heads = groups * taken
    keys = query.shape[2] * (len(far) + 2)
    flops = heads * SAMPLE_COUNT * rows * HEAD_SIZE * (4 * keys + 12 * QUERY_TOKENS)
    return pl.pallas_call(
        functools.partial(head_kernel, len(far), earlier is not None),
        grid=(heads,),
        in_specs=in_specs,
        out_specs=[
            whole,
            whole,
            pl.BlockSpec(
                (1, 2, QUERY_TOKENS, HEAD_SIZE), lambda i: (i // taken, 0, 0, i % taken)
            ),
        ],
        out_shape=[
            jax.ShapeDtypeStruct(query.shape, jnp.bfloat16),
            jax.ShapeDtypeStruct(query.shape, jnp.bfloat16),
            jax.ShapeDtypeStruct((groups, 2, QUERY_TOKENS, taken * HEAD_SIZE), jnp.bfloat16),
        ],
        input_output_aliases=aliases,
        compiler_params=pltpu.CompilerParams(vmem_limit_bytes=40 * 1024 * 1024),
        cost_estimate=pl.CostEstimate(
            flops=4 * flops,
            bytes_accessed=heads * rows * HEAD_SIZE * 24,
            transcendentals=heads * SAMPLE_COUNT * rows * keys,
        ),
    )(*operands)


def head_pieces(per_group):
    pieces, start = [], 0
    while start < per_group:
        taken = max(1, (per_group - start) // 3)
        pieces.append((start, taken))
        start += taken
    return pieces


MESH = pl.DeviceIdType.MESH
DEPTH = 4
STEPS = (6, 7, 11, 12, 16, 17)


def self_head(query_of, keys_of, values_of):
    pieces = []
    for sample in range(SAMPLE_COUNT):
        scores = [mm(query_of(sample), key, NT) for key in keys_of(sample)]
        top = jnp.max(functools.reduce(jnp.maximum, scores), axis=1, keepdims=True)
        terms = [jnp.exp((s - top) * score_scale) for s in scores]
        total = jnp.sum(functools.reduce(jnp.add, terms), axis=1, keepdims=True)
        mixed = functools.reduce(
            jnp.add, [mm(e.astype(jnp.bfloat16), v, NN) for e, v in zip(terms, values_of(sample))]
        )
        pieces.append((mixed / total).astype(jnp.bfloat16))
    return pieces


def cross_head(latent, context_keys, condition_values, gradient):
    latent = latent.astype(jnp.float32)
    inverse = lax.rsqrt(jnp.mean(latent * latent, axis=1, keepdims=True) + norm_eps)
    normed = latent * inverse
    query_round = normed.astype(jnp.bfloat16)
    key_float = context_keys.astype(jnp.float32)
    key_inverse = lax.rsqrt(jnp.mean(key_float * key_float, axis=1, keepdims=True) + norm_eps)
    key_normed = key_float * key_inverse
    key_round = key_normed.astype(jnp.bfloat16)
    exp_terms = jnp.exp(mm(key_round, query_round, NT) * score_scale)
    weights = exp_terms / jnp.sum(exp_terms, axis=0, keepdims=True)
    weights_round = weights.astype(jnp.bfloat16)
    out = latent + mm(weights_round, condition_values, TN)
    value_gradient = mm(weights_round, gradient, NN)
    weight_grad = mm(condition_values, gradient, NT)
    delta = jnp.sum(weights * weight_grad, axis=0, keepdims=True)
    score_grad = (weights * (weight_grad - delta) * score_scale).astype(jnp.bfloat16)
    query_grad = mm(score_grad, key_round, TN)
    key_grad = mm(score_grad, query_round, NN)
    grad = gradient.astype(jnp.float32) + inverse * (
        query_grad - normed * jnp.mean(query_grad * normed, axis=1, keepdims=True)
    )
    key_grad = key_inverse * (
        key_grad - key_normed * jnp.mean(key_grad * key_normed, axis=1, keepdims=True)
    )
    return tuple(a.astype(jnp.bfloat16) for a in (out, grad, key_grad, value_gradient))


def whole_kernel(
    size,
    prompts,
    llm_query_ref,
    llm_kv_ref,
    connector_ref,
    query_ref,
    key_ref,
    value_ref,
    cotangent_ref,
    out_ref,
    grad_ref,
    context_grad_ref,
    kv,
    q_all,
    g_all,
    latent,
    llm_q,
    llm_parts,
    connector,
    hidden,
    partial,
    sum_out,
    sum_in,
    half,
    half_out,
    half_in,
    mine,
    context,
    pg,
    pg_near,
    pg_out,
    pg_far,
    load_sem,
    whole_sem,
    far_send,
    far_recv,
    near_send,
    near_recv,
    pass_send,
    pass_recv,
    llm_send,
    llm_recv,
    hidden_send,
    hidden_recv,
    sum_send,
    sum_recv,
    token_send,
    token_recv,
    gather_send,
    gather_recv,
    pg_send,
    pg_recv,
    out_sem,
):
    me = lax.axis_index("tp")
    row = lax.axis_index("fsdp")
    core = me % 2
    half_index = me // 2
    near = me + 1 - 2 * core
    far = me + 2 - 4 * half_index
    heads = DENOISER_HEADS
    per = heads // size
    rows = query_ref.shape[2]
    block = QUERY_TOKENS // size
    llm_width = llm_parts.shape[3]
    columns = connector_ref.shape[1]
    bf = jnp.bfloat16

    def peer_at(distance):
        low, high = distance % 2, distance // 2
        new_core = core + low - 2 * core * low
        new_half = half_index + high - 2 * half_index * high
        return new_half * 2 + new_core

    def remote(src, dst, send, recv, **where):
        return pltpu.make_async_remote_copy(
            src_ref=src,
            dst_ref=dst,
            send_sem=send,
            recv_sem=recv,
            device_id=where,
            device_id_type=MESH,
        )

    def head_of(i):
        return (i % size) * per + i // size

    def cols(i):
        return pl.ds(pl.multiple_of(head_of(i) * HEAD_SIZE, HEAD_SIZE), HEAD_SIZE)

    def load(i, which):
        source = (key_ref, value_ref)[which]
        return pltpu.make_async_copy(
            source.at[0, :, :, cols(i)], kv.at[0, i, which], load_sem.at[i, which]
        )

    def far_copy(i):
        return remote(kv.at[0, i], kv.at[2, i], far_send.at[i], far_recv.at[i], tp=far)

    def near_copy(i):
        return remote(kv.at[0, i], kv.at[1, i], near_send.at[i], near_recv.at[i], tp=near)

    def pass_copy(i):
        return remote(kv.at[2, i], kv.at[3, i], pass_send.at[i], pass_recv.at[i], tp=near)

    def llm_copy(d):
        start = pl.multiple_of(peer_at(d) * llm_width, HEAD_SIZE)
        return remote(
            llm_kv_ref.at[0, :, :, pl.ds(start, llm_width)],
            llm_parts.at[me],
            llm_send.at[d - 1],
            llm_recv.at[d - 1],
            tp=peer_at(d),
        )

    def llm_came(d):
        there = llm_parts.at[peer_at(d)]
        return remote(there, there, llm_send.at[d - 1], llm_recv.at[d - 1], tp=peer_at(d))

    own_start = pl.multiple_of(me * llm_width, HEAD_SIZE)
    llm_q_load = pltpu.make_async_copy(llm_query_ref.at[0], llm_q, whole_sem.at[0])
    llm_own_load = pltpu.make_async_copy(
        llm_kv_ref.at[0, :, :, pl.ds(own_start, llm_width)], llm_parts.at[me], whole_sem.at[1]
    )
    q_load = pltpu.make_async_copy(query_ref.at[0], q_all, whole_sem.at[2])
    g_load = pltpu.make_async_copy(cotangent_ref.at[0], g_all, whole_sem.at[3])
    connector_load = pltpu.make_async_copy(connector_ref, connector, whole_sem.at[4])

    llm_q_load.start()
    llm_own_load.start()

    @pl.loop(0, heads)
    def _(i):
        load(i, 0).start()
        load(i, 1).start()

    q_load.start()
    connector_load.start()
    g_load.start()

    barrier = pltpu.get_barrier_semaphore()
    for d in range(1, size):
        pl.semaphore_signal(barrier, inc=1, device_id={"tp": peer_at(d)}, device_id_type=MESH)
    for d in range(1, prompts):
        pl.semaphore_signal(
            barrier, inc=1, device_id={"fsdp": (row + d) % prompts}, device_id_type=MESH
        )
    pl.semaphore_wait(barrier, size - 1 + prompts - 1)

    for d in range(size - 1, 0, -1):
        llm_copy(d).start()

    @pl.loop(0, DEPTH)
    def _(i):
        load(i, 0).wait()
        load(i, 1).wait()
        far_copy(i).start()
        near_copy(i).start()

    @pl.loop(DEPTH, heads)
    def _(i):
        load(i, 0).wait()
        load(i, 1).wait()
        near_copy(i).start()

    llm_q_load.wait()
    llm_own_load.wait()
    for d in range(1, size):
        llm_came(d).wait_recv()
    kv_heads = llm_width // HEAD_SIZE
    group = llm_q.shape[1] // llm_width
    positions = size * llm_parts.shape[2]
    shape = (group * QUERY_TOKENS, positions)
    token = lax.broadcasted_iota(jnp.int32, shape, 0) % QUERY_TOKENS
    allowed = lax.broadcasted_iota(jnp.int32, shape, 1) <= PROMPT + token
    for k in range(kv_heads):
        at = slice(k * HEAD_SIZE, (k + 1) * HEAD_SIZE)
        base = k * group * HEAD_SIZE
        stacked = jnp.concatenate(
            [llm_q[:, base + j * HEAD_SIZE : base + (j + 1) * HEAD_SIZE] for j in range(group)], 0
        )
        keys = jnp.concatenate([llm_parts[j, 0, :, at] for j in range(size)], 0)
        values = jnp.concatenate([llm_parts[j, 1, :, at] for j in range(size)], 0)
        scores = jnp.where(allowed, mm(stacked, keys, NT) * score_scale, -1e30)
        terms = jnp.exp(scores - jnp.max(scores, axis=1, keepdims=True))
        total = jnp.sum(terms, axis=1, keepdims=True)
        mixed = (mm((terms / total).astype(bf), values, NN)).astype(bf)
        for j in range(group):
            hidden[row, :, base + j * HEAD_SIZE : base + (j + 1) * HEAD_SIZE] = mixed[
                j * QUERY_TOKENS : (j + 1) * QUERY_TOKENS
            ]

    def hidden_copy(d):
        return remote(
            hidden.at[row],
            hidden.at[row],
            hidden_send.at[d - 1],
            hidden_recv.at[d - 1],
            fsdp=(row + d) % prompts,
        )

    def hidden_came(d):
        there = hidden.at[(row + prompts - d) % prompts]
        return remote(
            there,
            there,
            hidden_send.at[d - 1],
            hidden_recv.at[d - 1],
            fsdp=(row + d) % prompts,
        )

    for d in range(1, prompts):
        hidden_copy(d).start()

    sum_copy = remote(sum_out, sum_in, sum_send.at[0], sum_recv.at[0], tp=near)
    half_copy = remote(half_out, half_in, sum_send.at[1], sum_recv.at[1], tp=far)

    def project():
        for d in range(1, prompts):
            hidden_came(d).wait_recv()
        connector_load.wait()
        rows_in = hidden[...].reshape(prompts * QUERY_TOKENS, hidden.shape[2])
        tile = HEAD_SIZE

        @pl.loop(0, columns // tile)
        def _(c):
            at = pl.ds(pl.multiple_of(c * tile, tile), tile)
            product = mm(rows_in, connector[:, at], NN)
            partial[:, :, :, at] = product.reshape(prompts, size, block, tile)

        for h in range(2):
            sum_out[h] = partial[:, 2 * h + 1 - core].astype(bf)
        sum_copy.start()

    def halve():
        sum_copy.wait_recv()
        half[...] = partial[:, 2 * half_index + core] + sum_in[half_index].astype(jnp.float32)
        other = 1 - half_index
        half_out[...] = (partial[:, 2 * other + core] + sum_in[other].astype(jnp.float32)).astype(bf)
        half_copy.start()

    def token_copy(d):
        to = (row + d) % prompts
        return remote(
            mine.at[to], context.at[me, row], token_send.at[d - 1], token_recv.at[d - 1], fsdp=to
        )

    def token_came(d):
        there = context.at[me, (row + prompts - d) % prompts]
        return remote(
            there,
            there,
            token_send.at[d - 1],
            token_recv.at[d - 1],
            fsdp=(row + d) % prompts,
        )

    def spread():
        half_copy.wait_recv()
        mine[...] = (half[...] + half_in[...].astype(jnp.float32)).astype(bf)
        context[me, row] = mine[row]
        for d in range(1, prompts):
            token_copy(d).start()

    def gather_copy(k, who, to):
        return remote(context.at[who], context.at[who], gather_send.at[k], gather_recv.at[k], tp=to)

    def gather_far():
        for d in range(1, prompts):
            token_came(d).wait_recv()
        gather_copy(0, me, far).start()
        gather_copy(1, me, near).start()

    def gather_near():
        gather_copy(0, far, far).wait_recv()
        gather_copy(2, far, near).start()

    def gathered():
        gather_copy(1, near, near).wait_recv()
        gather_copy(2, peer_at(3), near).wait_recv()
        g_load.wait()

    def condition(position):
        at = pl.ds(pl.multiple_of(position % columns, HEAD_SIZE), HEAD_SIZE)
        return context[:, position // columns, :, at].reshape(QUERY_TOKENS, HEAD_SIZE)

    def out_copy(i, which):
        if which == 0:
            source, target = latent.at[i], out_ref
        else:
            source, target = g_all.at[:, :, cols(i)], grad_ref
        return pltpu.make_async_copy(source, target.at[0, :, :, cols(i)], out_sem.at[i, which])

    def cross(i):
        start = head_of(i) * HEAD_SIZE
        out, grad, key_grad, value_gradient = cross_head(
            latent[i].reshape(SAMPLE_COUNT * rows, HEAD_SIZE),
            condition(start),
            condition(heads * HEAD_SIZE + start),
            g_all[:, :, cols(i)].reshape(SAMPLE_COUNT * rows, HEAD_SIZE),
        )
        latent[i] = out.reshape(SAMPLE_COUNT, rows, HEAD_SIZE)
        g_all[:, :, cols(i)] = grad.reshape(SAMPLE_COUNT, rows, HEAD_SIZE)
        out_copy(i, 0).start()
        out_copy(i, 1).start()
        pg[i % size, i // size, 0] = key_grad
        pg[i % size, i // size, 1] = value_gradient

    batches = ((0, per - 1), (per - 1, 1))

    def pg_near_copy(b, h):
        at = pl.ds(*batches[b])
        return remote(
            pg.at[2 * h + 1 - core, at],
            pg_near.at[h, at],
            pg_send.at[3 * b + h],
            pg_recv.at[3 * b + h],
            tp=near,
        )

    def pg_far_copy(b):
        at = pl.ds(*batches[b])
        return remote(
            pg_out.at[at], pg_far.at[at], pg_send.at[3 * b + 2], pg_recv.at[3 * b + 2], tp=far
        )

    def pg_start(b):
        for h in range(2):
            pg_near_copy(b, h).start()

    def pg_middle(b):
        for h in range(2):
            pg_near_copy(b, h).wait_recv()
        at = pl.ds(*batches[b])
        other = 1 - half_index
        total = pg[2 * other + core, at].astype(jnp.float32) + pg_near[other, at].astype(jnp.float32)
        pg_out[at] = total.astype(bf)
        pg_far_copy(b).start()

    def pg_end(b):
        pg_far_copy(b).wait_recv()
        first, count = batches[b]
        for s in range(first, first + count):
            total = (
                pg[me, s].astype(jnp.float32)
                + pg_near[half_index, s].astype(jnp.float32)
                + pg_far[s].astype(jnp.float32)
            )
            context_grad_ref[0, :, :, s * HEAD_SIZE : (s + 1) * HEAD_SIZE] = total.astype(bf)

    q_load.wait()
    ready = STEPS[5] * heads // 24
    rate = -(-heads // (heads - ready - 1))
    sent = next(
        i for i in range(ready, heads) if min(rate * (i - ready + 1), i) >= size * (per - 1)
    )

    @pl.loop(0, heads)
    def _(i):
        far_copy(i).wait_recv()
        pass_copy(i).start()

        @pl.when(i + DEPTH < heads)
        def _():
            far_copy(i + DEPTH).start()

        near_copy(i).wait_recv()
        works = (project, halve, spread, gather_far, gather_near, gathered)
        for at, work in zip(STEPS, works):
            pl.when(i == at * heads // 24)(work)
        if sent + 1 < heads:
            pl.when(i == sent + 1)(functools.partial(pg_middle, 0))

        first = jnp.where(i < ready, i, jnp.minimum(rate * (i - ready), i - 1))
        last = jnp.where(i < ready, i, jnp.minimum(rate * (i - ready + 1), i))

        @pl.loop(first, last)
        def _(c):
            cross(c)

        @pl.when(i == sent)
        def _():
            pg_start(0)

        pass_copy(i).wait_recv()

        def part(which):
            def of(sample):
                return [kv[source, i, which, sample] for source in range(size)]

            return of

        pieces = self_head(lambda sample: q_all[sample, :, cols(i)], part(0), part(1))
        for sample in range(SAMPLE_COUNT):
            latent[i, sample] = pieces[sample]

    cross(heads - 1)
    if sent + 1 >= heads:
        pg_middle(0)
    pg_start(1)
    pg_end(0)
    pg_middle(1)
    pg_end(1)

    @pl.loop(0, heads)
    def _(i):
        far_copy(i).wait_send()
        near_copy(i).wait_send()
        pass_copy(i).wait_send()
        out_copy(i, 0).wait()
        out_copy(i, 1).wait()

    for d in range(1, size):
        llm_copy(d).wait_send()
    for d in range(1, prompts):
        hidden_copy(d).wait_send()
        token_copy(d).wait_send()
    sum_copy.wait_send()
    half_copy.wait_send()
    gather_copy(0, me, far).wait_send()
    gather_copy(1, me, near).wait_send()
    gather_copy(2, far, near).wait_send()
    for b in range(2):
        for h in range(2):
            pg_near_copy(b, h).wait_send()
        pg_far_copy(b).wait_send()


def whole_call(arrays):
    llm_query, llm_kv, connector, self_query, self_key, latent_value, cotangent = arrays
    size = lax.axis_size("tp")
    prompts = lax.axis_size("fsdp")
    heads = DENOISER_HEADS
    per = heads // size
    rows = self_query.shape[2]
    block = QUERY_TOKENS // size
    columns = connector.shape[1]
    llm_width = llm_query.shape[2] // (LLM_HEADS // LLM_KV)
    bf = jnp.bfloat16
    dma = pltpu.SemaphoreType.DMA
    width = heads * HEAD_SIZE
    any_space = pl.BlockSpec(memory_space=pl.ANY)
    token_block = (prompts, block, columns)
    return pl.pallas_call(
        functools.partial(whole_kernel, size, prompts),
        in_specs=[any_space] * 7,
        out_specs=[any_space, any_space, pl.BlockSpec(memory_space=pltpu.VMEM)],
        out_shape=[
            jax.ShapeDtypeStruct(self_query.shape, bf),
            jax.ShapeDtypeStruct(self_query.shape, bf),
            jax.ShapeDtypeStruct((1, 2, QUERY_TOKENS, per * HEAD_SIZE), bf),
        ],
        scratch_shapes=[
            pltpu.VMEM((size, heads, 2, SAMPLE_COUNT, rows, HEAD_SIZE), bf),
            pltpu.VMEM((SAMPLE_COUNT, rows, width), bf),
            pltpu.VMEM((SAMPLE_COUNT, rows, width), bf),
            pltpu.VMEM((heads, SAMPLE_COUNT, rows, HEAD_SIZE), bf),
            pltpu.VMEM(llm_query.shape[1:], bf),
            pltpu.VMEM((size, 2, llm_kv.shape[2], llm_width), bf),
            pltpu.VMEM(connector.shape, bf),
            pltpu.VMEM((prompts, QUERY_TOKENS, llm_query.shape[2]), bf),
            pltpu.VMEM((prompts, size, block, columns), jnp.float32),
            pltpu.VMEM((2,) + token_block, bf),
            pltpu.VMEM((2,) + token_block, bf),
            pltpu.VMEM(token_block, jnp.float32),
            pltpu.VMEM(token_block, bf),
            pltpu.VMEM(token_block, bf),
            pltpu.VMEM(token_block, bf),
            pltpu.VMEM((size,) + token_block, bf),
            pltpu.VMEM((size, per, 2, QUERY_TOKENS, HEAD_SIZE), bf),
            pltpu.VMEM((2, per, 2, QUERY_TOKENS, HEAD_SIZE), bf),
            pltpu.VMEM((per, 2, QUERY_TOKENS, HEAD_SIZE), bf),
            pltpu.VMEM((per, 2, QUERY_TOKENS, HEAD_SIZE), bf),
            dma((heads, 2)),
            dma((5,)),
            dma((heads,)),
            dma((heads,)),
            dma((heads,)),
            dma((heads,)),
            dma((heads,)),
            dma((heads,)),
            dma((size - 1,)),
            dma((size - 1,)),
            dma((prompts - 1,)),
            dma((prompts - 1,)),
            dma((2,)),
            dma((2,)),
            dma((prompts - 1,)),
            dma((prompts - 1,)),
            dma((3,)),
            dma((3,)),
            dma((6,)),
            dma((6,)),
            dma((heads, 2)),
        ],
        compiler_params=pltpu.CompilerParams(
            collective_id=0, has_side_effects=True, vmem_limit_bytes=60 * 1024 * 1024
        ),
        cost_estimate=pl.CostEstimate(
            flops=10**10, bytes_accessed=23 * 10**6, transcendentals=10**7
        ),
    )(*arrays)


def one_kernel_fits(connector):
    size = lax.axis_size("tp")
    return (
        len(tp_masks()) == 2
        and DENOISER_HEADS % size == 0
        and LLM_KV % size == 0
        and QUERY_TOKENS % (16 * size) == 0
        and connector.shape[1] % HEAD_SIZE == 0
    )


def shards(llm_query, llm_kv, connector, self_query, self_key, latent_value, cotangent):
    if one_kernel_fits(connector):
        return whole_call(
            (llm_query, llm_kv, connector, self_query, self_key, latent_value, cotangent)
        )
    size = lax.axis_size("tp")
    groups = math.gcd(DENOISER_HEADS, size)
    masks = tp_masks()
    pieces = head_pieces(DENOISER_HEADS // groups)
    rows = self_query.shape[2]

    def piece_of(array, start, taken):
        array = array.reshape(SAMPLE_COUNT, rows, groups, -1, HEAD_SIZE)
        array = array[:, :, :, start : start + taken]
        return array.reshape(SAMPLE_COUNT, rows, groups * taken * HEAD_SIZE)

    far_parts = []
    for start, taken in pieces:
        parts = [
            jnp.stack([piece_of(self_key, start, taken), piece_of(latent_value, start, taken)])
        ]
        for mask in masks[:-1]:
            parts += [exchange(part, mask) for part in parts]
        far_parts.append(parts[1:])
    near = [
        self_key,
        exchange(self_key, masks[-1]),
        latent_value,
        exchange(latent_value, masks[-1]),
    ]
    context = context_of(llm_query, llm_kv, connector)
    earlier = None
    context_pieces = []
    for (start, taken), parts in zip(pieces, far_parts):
        far = parts + [exchange(part, masks[-1]) for part in parts]
        latent_out, self_grad, partial = attend(
            groups, start, taken, self_query, cotangent, context, near, far, earlier
        )
        earlier = (latent_out, self_grad)
        if groups == size:
            partial = reduce_scatter(partial).astype(jnp.bfloat16)
        context_pieces.append(partial)
    context_grad = jnp.concatenate(context_pieces, axis=-1)
    if groups == size:
        context_grad = context_grad[None]
    else:
        context_grad = context_grad.transpose(1, 2, 0, 3).reshape(1, 2, QUERY_TOKENS, -1)
        context_grad = lax.psum_scatter(context_grad, "tp", scatter_dimension=3, tiled=True)
    return (latent_out, self_grad, context_grad)


def solution(mesh):
    placed = (
        P("fsdp", None, "tp"),
        P("fsdp", None, "tp", None),
        P("tp", "fsdp"),
        P("fsdp", None, "tp", None),
        P("fsdp", None, "tp", None),
        P("fsdp", None, "tp", None),
        P("fsdp", None, "tp", None),
    )
    return jax.shard_map(
        shards,
        mesh=mesh,
        in_specs=placed,
        out_specs=(
            P("fsdp", None, "tp", None),
            P("fsdp", None, "tp", None),
            P("fsdp", None, None, "tp"),
        ),
        check_vma=False,
    )
```
